32 devices in a mesh: group: 16 (over z, y, x), head: 2 (over core).
Axes of the slice: x: 2, y: 2, z: 4, core: 2. Of those that a mesh axis runs over, the one named last changes fastest.
Arguments:
- queries: bfloat16 [256, 8, 64, 128], P('group', None, 'head'), may hold values from -12 to 12
- fresh_kv: bfloat16 [256, 8, 8, 2, 128], P('group', None, 'head'), may hold values from -4 to 4
- page_pool: bfloat16 [1024, 8, 2, 128, 128], P('group', 'head'), may hold values from -6 to 6
- context_len: int32 [256], P('group'), may hold values from 1 to 1024, as said below
- page_holder: int32 [256, 8], P('group'), may hold values from 0 to 15, as said below
- page_index: int32 [256, 8], P('group'), may hold values from 0 to 63
- hot_owner: int32 [1], replicated, may hold values from 0 to 15
- hot_pages: int32 [32], replicated, may hold values from 0 to 63
Outputs:
- attended: bfloat16 [256, 8, 64, 128], P('group', None, 'head')
The draws below stay inside these ranges and needn't reach their ends.
Inputs may be any that keep to these rules, and one draw needn't show every extreme that they name: `context_len`: in each decode group of 16 requests one request has exactly 1024 tokens. `page_holder`: among the entries of one decode group's 16 requests each holder group is named at most 8 times; entries of pages past a request's context are not read.
All inputs are finite; a program needn't handle non-finite values.
Results may differ from the reference program's by a relative error of at most 0.02.
Values may be sent and summed in bfloat16 or wider, within the bound.
A program may use at most 192 MiB of HBM per device.

```python
import math
import jax
import jax.numpy as jnp
from jax import lax

HD = 128
QH = 64
KVH = 8
PAGE = 128
STEPS = 8
HOTP = 32
MAXP = 8
POOL = 64
REQ = 16
REQS = 256
CAP = 8
N_GROUP = 16


def draw_queries(key, part):
    key = jax.random.fold_in(key, 11)
    drawn = 2.5 * jax.random.truncated_normal(key, -4.8, 4.8, (REQS, STEPS, QH, HD), jnp.float32)
    return drawn.astype(jnp.bfloat16)


def draw_fresh_kv(key, part):
    key = jax.random.fold_in(key, 23)
    drawn = jax.random.truncated_normal(key, -4.0, 4.0, (REQS, STEPS, KVH, 2, HD), jnp.float32)
    return drawn.astype(jnp.bfloat16)


def draw_context_len(key, part):
    key = jax.random.fold_in(key, 31)
    len_key, pick_key = jax.random.split(key)
    longest = MAXP * PAGE
    drawn = jax.random.randint(len_key, (N_GROUP, REQ), 1, longest + 1)
    longest_at = jax.random.randint(pick_key, (N_GROUP, 1), 0, REQ)
    drawn = jnp.where(jnp.arange(REQ)[None, :] == longest_at, longest, drawn)
    return drawn.reshape(REQS).astype(jnp.int32)


def one_order(group_key):
    return jax.random.permutation(group_key, N_GROUP)


def draw_page_holder(key, part):
    key = jax.random.fold_in(key, 47)
    orders = jax.vmap(one_order)(jax.random.split(key, N_GROUP))
    slot_owner = jnp.arange(REQ * MAXP) // CAP
    holders = orders[:, slot_owner]
    return holders.reshape(REQS, MAXP).astype(jnp.int32)


def place_ends(values, own_key, low, largest):
    longest = values.shape.index(max(values.shape))
    spots = []
    for shift in (0, 1):
        where = [jax.random.randint(jax.random.fold_in(own_key, axis), (), 0, length) for axis, length in enumerate(values.shape)]
        where[longest] = (where[longest] + shift) % values.shape[longest]
        spots.append(tuple(where))
    return values.at[spots[0]].set(low).at[spots[1]].set(largest)


def block_levels(rng, shape, pieces, low, top_value):
    factor_of = 1.0
    for dim, blocks in pieces:
        steps = jax.random.uniform(jax.random.fold_in(jax.random.fold_in(rng, 6), dim), (blocks,), jnp.float32, low / len(pieces), top_value / len(pieces))
        factor_of = factor_of * jnp.repeat(jnp.exp(steps), shape[dim] // blocks).reshape((-1,) + (1,) * (len(shape) - 1 - dim))
    return factor_of


def bell_draw(key, shape, deviation, most, pieces=(), kind=jnp.bfloat16):
    entries = jax.random.normal(key, shape, jnp.float32) * deviation
    if len(pieces) > 0:
        entries = block_levels(key, shape, pieces, -0.22, 0.18) * entries
    return jnp.clip(entries, min=-most, max=most).astype(kind)


def setup_inputs(seed: int = 0) -> dict:
    seeds = jax.random.split(jax.random.key(seed), 9)
    queries = draw_queries(jax.random.fold_in(seeds[8], 71), 0)
    fresh_kv = draw_fresh_kv(jax.random.fold_in(seeds[8], 71), 0)
    page_pool = bell_draw(seeds[2], (N_GROUP * POOL, KVH, 2, PAGE, HD), 1.0, 6.0, ((0, 16), (1, 2)))
    context_len = draw_context_len(jax.random.fold_in(seeds[8], 71), 0)
    page_holder = draw_page_holder(jax.random.fold_in(seeds[8], 71), 0)
    page_index = place_ends(jax.random.randint(seeds[5], (REQS, MAXP), 0, POOL), jax.random.fold_in(seeds[5], 1), 0, POOL - 1).astype(jnp.int32)
    hot_owner = jax.random.randint(seeds[6], (1,), 0, N_GROUP).astype(jnp.int32)
    hot_pages = place_ends(jax.random.randint(seeds[7], (HOTP,), 0, POOL), jax.random.fold_in(seeds[7], 1), 0, POOL - 1).astype(jnp.int32)
    return {"queries": queries, "fresh_kv": fresh_kv, "page_pool": page_pool, "context_len": context_len, "page_holder": page_holder, "page_index": page_index, "hot_owner": hot_owner, "hot_pages": hot_pages}


NEG_FILL = -1e+30

def rounded(weights):
    return lax.optimization_barrier(weights.astype(jnp.bfloat16)).astype(jnp.float32)

def reference(queries, fresh_kv, page_pool, context_len, page_holder, page_index, hot_owner, hot_pages):
    per_kv = QH // KVH
    score_scale = 1.0 / math.sqrt(HD)
    hot_kv = jnp.take(page_pool, hot_owner[0] * POOL + hot_pages, axis=0)
    hot_keys = hot_kv[:, :, 0].astype(jnp.float32)
    hot_values = hot_kv[:, :, 1].astype(jnp.float32)
    page_ids = (page_holder * POOL + page_index).astype(jnp.int32)
    token_order = jnp.arange(MAXP * PAGE, dtype=jnp.int32)
    step_order = jnp.arange(STEPS, dtype=jnp.int32)
    causal = step_order[None, :] <= step_order[:, None]

    def one_group(first_row):
        query_rows = lax.dynamic_slice_in_dim(queries, first_row, REQ, 0).astype(jnp.float32)
        query_rows = query_rows.reshape(REQ, STEPS, KVH, per_kv, HD)
        fresh_rows = lax.dynamic_slice_in_dim(fresh_kv, first_row, REQ, 0).astype(jnp.float32)
        lengths = lax.dynamic_slice_in_dim(context_len, first_row, REQ, 0)
        own_pages = jnp.take(page_pool, lax.dynamic_slice_in_dim(page_ids, first_row, REQ, 0), axis=0)
        private_keys = own_pages[:, :, :, 0].astype(jnp.float32).transpose(0, 2, 1, 3, 4).reshape(REQ, KVH, MAXP * PAGE, HD)
        private_values = own_pages[:, :, :, 1].astype(jnp.float32).transpose(0, 2, 1, 3, 4).reshape(REQ, KVH, MAXP * PAGE, HD)
        hot_scores = jnp.einsum('rsxgd,pxtd->rsxgpt', query_rows, hot_keys).reshape(REQ, STEPS, KVH, per_kv, HOTP * PAGE) * score_scale
        private_scores = jnp.einsum('rsxgd,rxkd->rsxgk', query_rows, private_keys) * score_scale
        fresh_scores = jnp.einsum('rsxgd,rkxd->rsxgk', query_rows, fresh_rows[:, :, :, 0]) * score_scale
        private_mask = (token_order[None, :] < lengths[:, None])[:, None, None, None, :]
        fresh_mask = causal[None, :, None, None, :]
        private_scores = jnp.where(private_mask, private_scores, NEG_FILL)
        fresh_scores = jnp.where(fresh_mask, fresh_scores, NEG_FILL)
        row_max = jnp.maximum(lax.optimization_barrier(jnp.max(hot_scores, axis=4)), jnp.maximum(lax.optimization_barrier(jnp.max(private_scores, axis=4)), lax.optimization_barrier(jnp.max(fresh_scores, axis=4))))
        hot_exp = jnp.exp(hot_scores - row_max[..., None])
        private_exp = jnp.where(private_mask, jnp.exp(private_scores - row_max[..., None]), 0.0)
        fresh_exp = jnp.where(fresh_mask, jnp.exp(fresh_scores - row_max[..., None]), 0.0)
        weight_sum = lax.optimization_barrier(jnp.sum(hot_exp, axis=4)) + lax.optimization_barrier(jnp.sum(private_exp, axis=4)) + lax.optimization_barrier(jnp.sum(fresh_exp, axis=4))
        weighted = jnp.einsum('rsxgpt,pxtd->rsxgd', rounded(hot_exp).reshape(REQ, STEPS, KVH, per_kv, HOTP, PAGE), hot_values)
        weighted = weighted + jnp.einsum('rsxgk,rxkd->rsxgd', rounded(private_exp), private_values)
        weighted = weighted + jnp.einsum('rsxgk,rkxd->rsxgd', rounded(fresh_exp), fresh_rows[:, :, :, 1])
        return (weighted / weight_sum[..., None]).astype(jnp.bfloat16).reshape(REQ, STEPS, QH, HD)
    blocks = lax.map(one_group, jnp.arange(N_GROUP, dtype=jnp.int32) * REQ)
    return blocks.reshape(REQS, STEPS, QH, HD)
```

```python
import functools
import math

import jax
import jax.numpy as jnp
from jax import lax
from jax.experimental import pallas as pl
from jax.experimental.pallas import tpu as pltpu
from jax.sharding import PartitionSpec as P

NEG_FILL = -1e30
VMEM_LIMIT = 48 * 1024 * 1024


def spread(value, axis, source):
    kept = jnp.where(lax.axis_index(axis) == source, value, 0).astype(value.dtype)
    return lax.psum(kept, axis)


def rows_by_keys(rows, keys):
    return lax.dot_general(rows, keys, (((1,), (1,)), ((), ())), preferred_element_type=jnp.float32)


def slot_kernel(capacity, kv_local, scale, ids_ref, fill_ref, q_ref, *refs):
    pages, (out_ref, lse_ref) = refs[:capacity], refs[capacity:]
    group = pl.program_id(0)
    rows, page_len = q_ref.shape[3], pages[0].shape[3]
    token = lax.broadcasted_iota(jnp.int32, (rows, page_len), 1)
    lane = lax.broadcasted_iota(jnp.int32, (rows, 128), 1)
    stats = jnp.full((rows, 128), NEG_FILL, jnp.float32)
    for c in range(capacity):
        allowed = token < fill_ref[group * capacity + c]
        for x in range(kv_local):
            scores = rows_by_keys(q_ref[0, c, x], pages[c][0, x, 0]) * scale
            scores = jnp.where(allowed, scores, NEG_FILL)
            top = jnp.max(scores, axis=1, keepdims=True)
            weights = jnp.where(allowed, jnp.exp(scores - top), 0.0)
            total = jnp.maximum(jnp.sum(weights, axis=1, keepdims=True), 1e-30)
            mixed = jnp.dot(
                weights.astype(jnp.bfloat16), pages[c][0, x, 1], preferred_element_type=jnp.float32
            )
            out_ref[0, c, x] = (mixed / total).astype(jnp.bfloat16)
            stats = jnp.where(lane == c * kv_local + x, top + jnp.log(total), stats)
    lse_ref[0] = stats


def slot_attention(slot_pages, slot_fill, slot_queries, page_pool, scale):
    groups, capacity, kv_local, rows, head_dim = slot_queries.shape
    page_len = page_pool.shape[3]

    def page_spec(c):
        return pl.BlockSpec(
            (1, kv_local, 2, page_len, head_dim),
            lambda g, ids, fill: (ids[g * capacity + c], 0, 0, 0, 0),
        )

    block = pl.BlockSpec((1, capacity, kv_local, rows, head_dim), lambda g, ids, fill: (g, 0, 0, 0, 0))
    flops = 4 * groups * capacity * kv_local * rows * page_len * head_dim
    return pl.pallas_call(
        functools.partial(slot_kernel, capacity, kv_local, scale),
        grid_spec=pltpu.PrefetchScalarGridSpec(
            num_scalar_prefetch=2,
            grid=(groups,),
            in_specs=[block] + [page_spec(c) for c in range(capacity)],
            out_specs=[block, pl.BlockSpec((1, rows, 128), lambda g, ids, fill: (g, 0, 0))],
        ),
        out_shape=[
            jax.ShapeDtypeStruct(slot_queries.shape, jnp.bfloat16),
            jax.ShapeDtypeStruct((groups, rows, 128), jnp.float32),
        ],
        compiler_params=pltpu.CompilerParams(vmem_limit_bytes=VMEM_LIMIT),
        cost_estimate=pl.CostEstimate(
            flops=flops, bytes_accessed=64 * 1024 * 1024, transcendentals=flops // (4 * head_dim)
        ),
        name="slot_attention",
    )(slot_pages, slot_fill, slot_queries, page_pool, *([page_pool] * (capacity - 1)))


def hot_kernel(scale, chunk, q_ref, hot_ref, out_ref, lse_ref):
    rows, head_dim = q_ref.shape[1], q_ref.shape[2]
    pages, page_len = hot_ref.shape[0], hot_ref.shape[3]
    q = q_ref[0]

    def step(i, carry):
        top, total, mixed = carry
        keys = hot_ref[pl.ds(i * chunk, chunk), 0, 0].reshape(chunk * page_len, head_dim)
        values = hot_ref[pl.ds(i * chunk, chunk), 0, 1].reshape(chunk * page_len, head_dim)
        scores = rows_by_keys(q, keys) * scale
        new_top = jnp.maximum(top, jnp.max(scores, axis=1, keepdims=True))
        weights = jnp.exp(scores - new_top)
        factor = jnp.exp(top - new_top)
        total = total * factor + jnp.sum(weights, axis=1, keepdims=True)
        mixed = mixed * factor + jnp.dot(
            weights.astype(jnp.bfloat16), values, preferred_element_type=jnp.float32
        )
        return new_top, total, mixed

    top, total, mixed = lax.fori_loop(
        0,
        pages // chunk,
        step,
        (
            jnp.full((rows, 1), NEG_FILL, jnp.float32),
            jnp.zeros((rows, 1), jnp.float32),
            jnp.zeros((rows, head_dim), jnp.float32),
        ),
        unroll=2,
    )
    out_ref[0] = mixed / total
    lse_ref[0] = jnp.broadcast_to(top + jnp.log(total), (rows, 128))


def hot_attention(query_rows, hot_kv, scale):
    kv_local, rows, head_dim = query_rows.shape
    pages, page_len = hot_kv.shape[0], hot_kv.shape[3]
    block = math.gcd(rows, 512)
    flops = 4 * kv_local * rows * pages * page_len * head_dim
    spec = pl.BlockSpec((1, block, head_dim), lambda x, m: (x, m, 0))
    return pl.pallas_call(
        functools.partial(hot_kernel, scale, math.gcd(pages, 4)),
        grid=(kv_local, rows // block),
        in_specs=[spec, pl.BlockSpec((pages, 1, 2, page_len, head_dim), lambda x, m: (0, x, 0, 0, 0))],
        out_specs=[spec, pl.BlockSpec((1, block, 128), lambda x, m: (x, m, 0))],
        out_shape=[
            jax.ShapeDtypeStruct((kv_local, rows, head_dim), jnp.float32),
            jax.ShapeDtypeStruct((kv_local, rows, 128), jnp.float32),
        ],
        compiler_params=pltpu.CompilerParams(vmem_limit_bytes=VMEM_LIMIT),
        cost_estimate=pl.CostEstimate(
            flops=flops, bytes_accessed=16 * 1024 * 1024, transcendentals=flops // (4 * head_dim)
        ),
        name="hot_attention",
    )(query_rows, hot_kv)


def join_kernel(
    max_pages, per_kv, scale, slot_ref, q_ref, fresh_ref, hot_ref, hot_lse_ref, lse_ref, *refs
):
    parts, out_ref = refs[:max_pages], refs[max_pages]
    kv_local, rows, _ = q_ref.shape[1:]
    steps = fresh_ref.shape[3]
    key_step = lax.broadcasted_iota(jnp.int32, (rows, steps), 1)
    row_step = lax.broadcasted_iota(jnp.int32, (rows, steps), 0) // per_kv
    causal = key_step <= row_step
    stats = lse_ref[0]
    for x in range(kv_local):
        fresh = rows_by_keys(q_ref[0, x], fresh_ref[0, x, 0]) * scale
        fresh = jnp.where(causal, fresh, NEG_FILL)
        hot_lse = hot_lse_ref[x][:, :1]
        cols = [stats[:, p * kv_local + x : p * kv_local + x + 1] for p in range(max_pages)]
        top = jnp.maximum(hot_lse, jnp.max(fresh, axis=1, keepdims=True))
        for col in cols:
            top = jnp.maximum(top, col)
        weights = jnp.where(causal, jnp.exp(fresh - top), 0.0)
        hot_weight = jnp.exp(hot_lse - top)
        total = jnp.sum(weights, axis=1, keepdims=True) + hot_weight
        mixed = hot_ref[x] * hot_weight + jnp.dot(
            weights.astype(jnp.bfloat16), fresh_ref[0, x, 1], preferred_element_type=jnp.float32
        )
        for p, col in enumerate(cols):
            share = jnp.exp(col - top)
            total = total + share
            mixed = mixed + parts[p][0, x].astype(jnp.float32) * share
        out_ref[0, x] = (mixed / total).astype(jnp.bfloat16)


def join(slot_of, query_rows, fresh_rows, hot_out, hot_lse, page_lse, parts, per_kv, scale):
    requests, kv_local, rows, head_dim = query_rows.shape
    max_pages = slot_of.shape[0] // requests
    steps = fresh_rows.shape[3]

    def part_spec(p):
        return pl.BlockSpec(
            (1, kv_local, rows, head_dim), lambda r, slot: (slot[r * max_pages + p], 0, 0, 0)
        )

    own = pl.BlockSpec((1, kv_local, rows, head_dim), lambda r, slot: (r, 0, 0, 0))
    return pl.pallas_call(
        functools.partial(join_kernel, max_pages, per_kv, scale),
        grid_spec=pltpu.PrefetchScalarGridSpec(
            num_scalar_prefetch=1,
            grid=(requests,),
            in_specs=[
                own,
                pl.BlockSpec((1, kv_local, 2, steps, head_dim), lambda r, slot: (r, 0, 0, 0, 0)),
                pl.BlockSpec((kv_local, rows, head_dim), lambda r, slot: (0, r, 0)),
                pl.BlockSpec((kv_local, rows, 128), lambda r, slot: (0, r, 0)),
                pl.BlockSpec((1, rows, 128), lambda r, slot: (r, 0, 0)),
            ]
            + [part_spec(p) for p in range(max_pages)],
            out_specs=own,
        ),
        out_shape=jax.ShapeDtypeStruct(query_rows.shape, jnp.bfloat16),
        compiler_params=pltpu.CompilerParams(vmem_limit_bytes=VMEM_LIMIT),
        name="join",
    )(slot_of, query_rows, fresh_rows, hot_out, hot_lse, page_lse, *([parts] * max_pages))


def on_device(
    queries, fresh_kv, page_pool, context_len, page_holder, page_index, hot_owner, hot_pages
):
    requests, steps, local_heads, head_dim = queries.shape
    kv_local = fresh_kv.shape[2]
    per_kv = local_heads // kv_local
    rows = steps * per_kv
    page_len = page_pool.shape[3]
    max_pages = page_holder.shape[1]
    groups = lax.axis_size("group")
    capacity = max(2, (requests * max_pages + groups - 1) // groups)
    slots = groups * capacity
    scale = 1.0 / math.sqrt(head_dim)

    query_rows = queries.reshape(requests, steps, kv_local, per_kv, head_dim)
    query_rows = query_rows.transpose(0, 2, 1, 3, 4).reshape(requests, kv_local, rows, head_dim)
    fresh_rows = fresh_kv.transpose(0, 2, 3, 1, 4)

    page_start = jnp.arange(max_pages, dtype=jnp.int32)[None, :] * page_len
    filled = jnp.clip(context_len[:, None] - page_start, 0, page_len).reshape(-1)
    live = filled > 0
    holder = page_holder.reshape(-1)
    member = (holder[:, None] == jnp.arange(groups, dtype=jnp.int32)[None, :]) & live[:, None]
    member = member.astype(jnp.int32)
    rank = jnp.sum((jnp.cumsum(member, axis=0) - member) * member, axis=1)
    slot_of = jnp.where(live, holder * capacity + rank, slots)
    taken = slot_of[None, :] == jnp.arange(slots, dtype=jnp.int32)[:, None]

    def by_slot(entry):
        return jnp.sum(jnp.where(taken, entry[None, :], 0), axis=1)

    entry_request = jnp.arange(requests * max_pages, dtype=jnp.int32) // max_pages
    slot_request = by_slot(entry_request)
    slot_info = jnp.stack([by_slot(page_index.reshape(-1)), by_slot(filled)], axis=1)
    slot_info = slot_info.reshape(groups, capacity, 2)

    asked = lax.all_to_all(slot_info, "group", split_axis=0, concat_axis=0, tiled=True)
    sent = jnp.take(query_rows, slot_request, axis=0)
    came = lax.all_to_all(
        sent.reshape(groups, capacity, kv_local, rows, head_dim),
        "group",
        split_axis=0,
        concat_axis=0,
        tiled=True,
    )
    hot_local = jnp.take(page_pool, hot_pages, axis=0)
    hot_kv = spread(hot_local, "group", hot_owner[0])
    asked = asked.reshape(slots, 2)
    part, part_lse = slot_attention(asked[:, 0], asked[:, 1], came, page_pool, scale)
    part = lax.all_to_all(part, "group", split_axis=0, concat_axis=0, tiled=True)
    part_lse = lax.all_to_all(part_lse, "group", split_axis=0, concat_axis=0, tiled=True)

    hot_rows = query_rows.transpose(1, 0, 2, 3).reshape(kv_local, requests * rows, head_dim)
    hot_out, hot_lse = hot_attention(hot_rows, hot_kv, scale)

    used = jnp.where(live, slot_of, 0)
    lse = part_lse[:, :, : capacity * kv_local].reshape(groups, rows, capacity, kv_local)
    lse = lse.transpose(0, 2, 1, 3).reshape(slots, rows, kv_local)
    lse = jnp.where(live[:, None, None], jnp.take(lse, used, axis=0), NEG_FILL)
    lse = lse.reshape(requests, max_pages, rows, kv_local).transpose(0, 2, 1, 3)
    lse = lse.reshape(requests, rows, max_pages * kv_local)
    lse = jnp.pad(lse, ((0, 0), (0, 0), (0, 128 - max_pages * kv_local)))
    part = part.reshape(slots, kv_local, rows, head_dim)
    attended = join(used, query_rows, fresh_rows, hot_out, hot_lse, lse, part, per_kv, scale)
    attended = attended.reshape(requests, kv_local, steps, per_kv, head_dim)
    return attended.transpose(0, 2, 1, 3, 4).reshape(requests, steps, local_heads, head_dim)


def solution(mesh):
    placed = (
        P("group", None, "head", None),
        P("group", None, "head", None, None),
        P("group", "head", None, None, None),
        P("group"),
        P("group", None),
        P("group", None),
        P(),
        P(),
    )
    return jax.shard_map(
        on_device,
        mesh=mesh,
        in_specs=placed,
        out_specs=P("group", None, "head", None),
        check_vma=False,
    )
```

```python
import functools
import math

import jax
import jax.numpy as jnp
from jax import lax
from jax.experimental import pallas as pl
from jax.experimental.pallas import tpu as pltpu
from jax.sharding import PartitionSpec as P

NEG_FILL = -1e30
VMEM_LIMIT = 48 * 1024 * 1024


def kept_by(value, axis, source):
    return jnp.where(lax.axis_index(axis) == source, value, 0).astype(value.dtype)


def rows_by_keys(rows, keys):
    return lax.dot_general(rows, keys, (((1,), (1,)), ((), ())), preferred_element_type=jnp.float32)


def slot_kernel(capacity, kv_local, scale, ids_ref, fill_ref, q_ref, *refs):
    pages, out_ref = refs[:capacity], refs[capacity]
    group = pl.program_id(0)
    rows, page_len = q_ref.shape[3], pages[0].shape[3]
    batch = math.gcd(capacity, 2)
    items = batch * kv_local
    token = lax.broadcasted_iota(jnp.int32, (rows, page_len), 1)
    lane = lax.broadcasted_iota(jnp.int32, (rows, 128), 1)
    stats = jnp.full((rows, 128), NEG_FILL, jnp.float32)
    for first in range(0, capacity, batch):
        pairs = [(c, x) for c in range(first, first + batch) for x in range(kv_local)]
        scores = []
        for c, x in pairs:
            allowed = token < fill_ref[group * capacity + c]
            score = rows_by_keys(q_ref[0, c, x], pages[c][0, x, 0]) * scale
            scores.append(jnp.where(allowed, score, NEG_FILL))
        scores = jnp.stack(scores)
        top = jnp.max(scores, axis=2, keepdims=True)
        weights = jnp.where(scores > 0.5 * NEG_FILL, jnp.exp(scores - top), 0.0)
        total = jnp.maximum(jnp.sum(weights, axis=2, keepdims=True), 1e-30)
        lse = top + jnp.log(total)
        inverse = 1.0 / total
        weights = weights.astype(jnp.bfloat16)
        for i in range(items):
            c, x = pairs[i]
            mixed = jnp.dot(weights[i], pages[c][0, x, 1], preferred_element_type=jnp.float32)
            out_ref[0, c * kv_local + x] = (mixed * inverse[i]).astype(jnp.bfloat16)
            stats = jnp.where(lane == c * kv_local + x, lse[i], stats)
    high = stats.astype(jnp.bfloat16)
    rest = stats - high.astype(jnp.float32)
    middle = rest.astype(jnp.bfloat16)
    low = (rest - middle.astype(jnp.float32)).astype(jnp.bfloat16)
    for i, term in enumerate((high, middle, low)):
        out_ref[0, capacity * kv_local + i] = term


def slot_attention(slot_pages, slot_fill, slot_queries, page_pool, scale):
    groups, capacity, kv_local, rows, head_dim = slot_queries.shape
    page_len = page_pool.shape[3]

    def page_spec(c):
        return pl.BlockSpec(
            (1, kv_local, 2, page_len, head_dim),
            lambda g, ids, fill: (ids[g * capacity + c], 0, 0, 0, 0),
        )

    block = pl.BlockSpec((1, capacity, kv_local, rows, head_dim), lambda g, ids, fill: (g, 0, 0, 0, 0))
    out_rows = capacity * kv_local + 3
    flops = 4 * groups * capacity * kv_local * rows * page_len * head_dim
    return pl.pallas_call(
        functools.partial(slot_kernel, capacity, kv_local, scale),
        grid_spec=pltpu.PrefetchScalarGridSpec(
            num_scalar_prefetch=2,
            grid=(groups,),
            in_specs=[block] + [page_spec(c) for c in range(capacity)],
            out_specs=pl.BlockSpec((1, out_rows, rows, head_dim), lambda g, ids, fill: (g, 0, 0, 0)),
        ),
        out_shape=jax.ShapeDtypeStruct((groups, out_rows, rows, head_dim), jnp.bfloat16),
        compiler_params=pltpu.CompilerParams(vmem_limit_bytes=VMEM_LIMIT),
        cost_estimate=pl.CostEstimate(
            flops=flops, bytes_accessed=64 * 1024 * 1024, transcendentals=flops // (4 * head_dim)
        ),
        name="slot_attention",
    )(slot_pages, slot_fill, slot_queries, page_pool, *([page_pool] * (capacity - 1)))


def hot_kernel(scale, chunk, q_ref, early_ref, late_ref, out_ref, lse_ref):
    rows, head_dim = q_ref.shape[1], q_ref.shape[2]
    pages, page_len = early_ref.shape[0], early_ref.shape[3]
    q = q_ref[0]

    def step(hot_ref, i, carry):
        top, total, mixed = carry
        keys = hot_ref[pl.ds(i * chunk, chunk), 0, 0].reshape(chunk * page_len, head_dim)
        values = hot_ref[pl.ds(i * chunk, chunk), 0, 1].reshape(chunk * page_len, head_dim)
        scores = rows_by_keys(q, keys) * scale
        new_top = jnp.maximum(top, jnp.max(scores, axis=1, keepdims=True))
        weights = jnp.exp(scores - new_top)
        factor = jnp.exp(top - new_top)
        total = total * factor + jnp.sum(weights, axis=1, keepdims=True)
        mixed = mixed * factor + jnp.dot(
            weights.astype(jnp.bfloat16), values, preferred_element_type=jnp.float32
        )
        return new_top, total, mixed

    carry = (
        jnp.full((rows, 1), NEG_FILL, jnp.float32),
        jnp.zeros((rows, 1), jnp.float32),
        jnp.zeros((rows, head_dim), jnp.float32),
    )
    for hot_ref in (early_ref, late_ref):
        carry = lax.fori_loop(
            0, pages // chunk, functools.partial(step, hot_ref), carry, unroll=2
        )
    top, total, mixed = carry
    out_ref[0] = mixed / total
    lse_ref[0] = jnp.broadcast_to(top + jnp.log(total), (rows, 128))


def hot_attention(query_rows, early, late, scale):
    kv_local, rows, head_dim = query_rows.shape
    pages, page_len = early.shape[0], early.shape[3]
    block = math.gcd(rows, 512)
    flops = 8 * kv_local * rows * pages * page_len * head_dim
    spec = pl.BlockSpec((1, block, head_dim), lambda x, m: (x, m, 0))
    half = pl.BlockSpec((pages, 1, 2, page_len, head_dim), lambda x, m: (0, x, 0, 0, 0))
    return pl.pallas_call(
        functools.partial(hot_kernel, scale, math.gcd(pages, 4)),
        grid=(kv_local, rows // block),
        in_specs=[spec, half, half],
        out_specs=[spec, pl.BlockSpec((1, block, 128), lambda x, m: (x, m, 0))],
        out_shape=[
            jax.ShapeDtypeStruct((kv_local, rows, head_dim), jnp.float32),
            jax.ShapeDtypeStruct((kv_local, rows, 128), jnp.float32),
        ],
        compiler_params=pltpu.CompilerParams(vmem_limit_bytes=VMEM_LIMIT),
        cost_estimate=pl.CostEstimate(
            flops=flops, bytes_accessed=16 * 1024 * 1024, transcendentals=flops // (4 * head_dim)
        ),
        name="hot_attention",
    )(query_rows, early, late)


def join_kernel(
    max_pages, per_kv, scale, slot_ref, q_ref, fresh_ref, hot_ref, hot_lse_ref, lse_ref, *refs
):
    parts, out_ref = refs[:max_pages], refs[max_pages]
    kv_local, rows, _ = q_ref.shape[1:]
    steps = fresh_ref.shape[3]
    key_step = lax.broadcasted_iota(jnp.int32, (rows, steps), 1)
    row_step = lax.broadcasted_iota(jnp.int32, (rows, steps), 0) // per_kv
    causal = key_step <= row_step
    stats = lse_ref[0]
    for x in range(kv_local):
        fresh = rows_by_keys(q_ref[0, x], fresh_ref[0, x, 0]) * scale
        fresh = jnp.where(causal, fresh, NEG_FILL)
        hot_lse = hot_lse_ref[x][:, :1]
        page_lse = stats[:, x * max_pages : (x + 1) * max_pages]
        top = jnp.maximum(hot_lse, jnp.max(fresh, axis=1, keepdims=True))
        top = jnp.maximum(top, jnp.max(page_lse, axis=1, keepdims=True))
        weights = jnp.where(causal, jnp.exp(fresh - top), 0.0)
        hot_weight = jnp.exp(hot_lse - top)
        shares = jnp.exp(page_lse - top)
        total = jnp.sum(weights, axis=1, keepdims=True) + hot_weight
        total = total + jnp.sum(shares, axis=1, keepdims=True)
        mixed = hot_ref[x] * hot_weight + jnp.dot(
            weights.astype(jnp.bfloat16), fresh_ref[0, x, 1], preferred_element_type=jnp.float32
        )
        for p in range(max_pages):
            mixed = mixed + parts[p][0, x].astype(jnp.float32) * shares[:, p : p + 1]
        out_ref[0, x] = (mixed / total).astype(jnp.bfloat16)


def join(capacity, slot_of, query_rows, fresh_rows, hot_out, hot_lse, page_lse, parts, per_kv, scale):
    requests, kv_local, rows, head_dim = query_rows.shape
    max_pages = slot_of.shape[0] // requests
    steps = fresh_rows.shape[3]

    def part_spec(p):
        return pl.BlockSpec(
            (1, kv_local, rows, head_dim),
            lambda r, slot: (
                lax.div(slot[r * max_pages + p], capacity),
                lax.rem(slot[r * max_pages + p], capacity),
                0,
                0,
            ),
        )

    own = pl.BlockSpec((1, kv_local, rows, head_dim), lambda r, slot: (r, 0, 0, 0))
    return pl.pallas_call(
        functools.partial(join_kernel, max_pages, per_kv, scale),
        grid_spec=pltpu.PrefetchScalarGridSpec(
            num_scalar_prefetch=1,
            grid=(requests,),
            in_specs=[
                own,
                pl.BlockSpec((1, kv_local, 2, steps, head_dim), lambda r, slot: (r, 0, 0, 0, 0)),
                pl.BlockSpec((kv_local, rows, head_dim), lambda r, slot: (0, r, 0)),
                pl.BlockSpec((kv_local, rows, 128), lambda r, slot: (0, r, 0)),
                pl.BlockSpec((1, rows, 128), lambda r, slot: (r, 0, 0)),
            ]
            + [part_spec(p) for p in range(max_pages)],
            out_specs=own,
        ),
        out_shape=jax.ShapeDtypeStruct(query_rows.shape, jnp.bfloat16),
        compiler_params=pltpu.CompilerParams(vmem_limit_bytes=VMEM_LIMIT),
        name="join",
    )(slot_of, query_rows, fresh_rows, hot_out, hot_lse, page_lse, *([parts] * max_pages))


def on_device(
    queries, fresh_kv, page_pool, context_len, page_holder, page_index, hot_owner, hot_pages
):
    requests, steps, local_heads, head_dim = queries.shape
    kv_local = fresh_kv.shape[2]
    per_kv = local_heads // kv_local
    rows = steps * per_kv
    page_len = page_pool.shape[3]
    max_pages = page_holder.shape[1]
    groups = lax.axis_size("group")
    capacity = max(2, (requests * max_pages + groups - 1) // groups)
    slots = groups * capacity
    scale = 1.0 / math.sqrt(head_dim)

    query_rows = queries.reshape(requests, steps, kv_local, per_kv, head_dim)
    query_rows = query_rows.transpose(0, 2, 1, 3, 4).reshape(requests, kv_local, rows, head_dim)
    fresh_rows = fresh_kv.transpose(0, 2, 3, 1, 4)

    page_start = jnp.arange(max_pages, dtype=jnp.int32)[None, :] * page_len
    filled = jnp.clip(context_len[:, None] - page_start, 0, page_len).reshape(-1)
    live = filled > 0
    holder = page_holder.reshape(-1)
    member = (holder[:, None] == jnp.arange(groups, dtype=jnp.int32)[None, :]) & live[:, None]
    member = member.astype(jnp.int32)
    rank = jnp.sum((jnp.cumsum(member, axis=0) - member) * member, axis=1)
    slot_of = jnp.where(live, holder * capacity + rank, slots)
    taken = slot_of[None, :] == jnp.arange(slots, dtype=jnp.int32)[:, None]

    def by_slot(entry):
        return jnp.sum(jnp.where(taken, entry[None, :], 0), axis=1)

    entry_request = jnp.arange(requests * max_pages, dtype=jnp.int32) // max_pages
    slot_request = by_slot(entry_request)
    slot_info = jnp.stack([by_slot(page_index.reshape(-1)), by_slot(filled)], axis=1)
    slot_info = slot_info.reshape(groups, capacity, 2)

    asked = lax.all_to_all(slot_info, "group", split_axis=0, concat_axis=0, tiled=True)
    sent = jnp.take(query_rows, slot_request, axis=0)
    came = lax.all_to_all(
        sent.reshape(groups, capacity, kv_local, rows, head_dim),
        "group",
        split_axis=0,
        concat_axis=0,
        tiled=True,
    )
    early, late = jnp.split(hot_pages, 2)
    early = kept_by(jnp.take(page_pool, early, axis=0), "group", hot_owner[0])
    late = kept_by(jnp.take(page_pool, late, axis=0), "group", hot_owner[0])
    early = lax.psum(early, "group")
    came, early, late = lax.optimization_barrier((came, early, late))
    late = lax.psum(late, "group")
    asked = asked.reshape(slots, 2)
    part = slot_attention(asked[:, 0], asked[:, 1], came, page_pool, scale)
    part, late = lax.optimization_barrier((part, late))
    part = lax.all_to_all(part, "group", split_axis=0, concat_axis=0, tiled=True)

    hot_rows = query_rows.transpose(1, 0, 2, 3).reshape(kv_local, requests * rows, head_dim)
    hot_out, hot_lse = hot_attention(hot_rows, early, late, scale)

    used = jnp.where(live, slot_of, 0)
    lse = jnp.sum(part[:, capacity * kv_local :].astype(jnp.float32), axis=1)
    lse = lse[:, :, : capacity * kv_local].reshape(groups, rows, capacity, kv_local)
    lse = lse.transpose(0, 2, 1, 3).reshape(slots, rows, kv_local)
    lse = jnp.where(live[:, None, None], jnp.take(lse, used, axis=0), NEG_FILL)
    lse = lse.reshape(requests, max_pages, rows, kv_local).transpose(0, 2, 3, 1)
    lse = lse.reshape(requests, rows, max_pages * kv_local)
    lse = jnp.pad(lse, ((0, 0), (0, 0), (0, 128 - max_pages * kv_local)))
    attended = join(
        capacity, used, query_rows, fresh_rows, hot_out, hot_lse, lse, part, per_kv, scale
    )
    attended = attended.reshape(requests, kv_local, steps, per_kv, head_dim)
    return attended.transpose(0, 2, 1, 3, 4).reshape(requests, steps, local_heads, head_dim)


def solution(mesh):
    placed = (
        P("group", None, "head", None),
        P("group", None, "head", None, None),
        P("group", "head", None, None, None),
        P("group"),
        P("group", None),
        P("group", None),
        P(),
        P(),
    )
    return jax.shard_map(
        on_device,
        mesh=mesh,
        in_specs=placed,
        out_specs=P("group", None, "head", None),
        check_vma=False,
    )
```

```python
import functools
import math

import jax
import jax.numpy as jnp
from jax import lax
from jax.experimental import pallas as pl
from jax.experimental.pallas import tpu as pltpu
from jax.sharding import PartitionSpec as P

NEG_FILL = -1e30
VMEM_LIMIT = 48 * 1024 * 1024


def kept_by(value, axis, source):
    return jnp.where(lax.axis_index(axis) == source, value, 0).astype(value.dtype)


def rows_by_keys(rows, keys):
    return lax.dot_general(rows, keys, (((1,), (1,)), ((), ())), preferred_element_type=jnp.float32)


def slot_kernel(capacity, kv_local, scale, ids_ref, fill_ref, q_ref, *refs):
    pages, out_ref = refs[:capacity], refs[capacity]
    group = pl.program_id(0)
    rows, page_len = q_ref.shape[3], pages[0].shape[3]
    batch = math.gcd(capacity, 2)
    items = batch * kv_local
    token = lax.broadcasted_iota(jnp.int32, (rows, page_len), 1)
    lane = lax.broadcasted_iota(jnp.int32, (rows, 128), 1)
    stats = jnp.full((rows, 128), NEG_FILL, jnp.float32)
    for first in range(0, capacity, batch):
        pairs = [(c, x) for c in range(first, first + batch) for x in range(kv_local)]
        scores = []
        for c, x in pairs:
            allowed = token < fill_ref[group * capacity + c]
            score = rows_by_keys(q_ref[0, c, x], pages[c][0, x, 0]) * scale
            scores.append(jnp.where(allowed, score, NEG_FILL))
        scores = jnp.stack(scores)
        top = jnp.max(scores, axis=2, keepdims=True)
        weights = jnp.where(scores > 0.5 * NEG_FILL, jnp.exp(scores - top), 0.0)
        total = jnp.maximum(jnp.sum(weights, axis=2, keepdims=True), 1e-30)
        lse = top + jnp.log(total)
        inverse = 1.0 / total
        weights = weights.astype(jnp.bfloat16)
        for i in range(items):
            c, x = pairs[i]
            mixed = jnp.dot(weights[i], pages[c][0, x, 1], preferred_element_type=jnp.float32)
            out_ref[0, c * kv_local + x] = (mixed * inverse[i]).astype(jnp.bfloat16)
            stats = jnp.where(lane == c * kv_local + x, lse[i], stats)
    high = stats.astype(jnp.bfloat16)
    rest = stats - high.astype(jnp.float32)
    middle = rest.astype(jnp.bfloat16)
    low = (rest - middle.astype(jnp.float32)).astype(jnp.bfloat16)
    for i, term in enumerate((high, middle, low)):
        out_ref[0, capacity * kv_local + i] = term


def slot_attention(slot_pages, slot_fill, slot_queries, page_pool, scale):
    groups, capacity, kv_local, rows, head_dim = slot_queries.shape
    page_len = page_pool.shape[3]

    def page_spec(c):
        return pl.BlockSpec(
            (1, kv_local, 2, page_len, head_dim),
            lambda g, ids, fill: (ids[g * capacity + c], 0, 0, 0, 0),
        )

    block = pl.BlockSpec((1, capacity, kv_local, rows, head_dim), lambda g, ids, fill: (g, 0, 0, 0, 0))
    out_rows = capacity * kv_local + 3
    flops = 4 * groups * capacity * kv_local * rows * page_len * head_dim
    return pl.pallas_call(
        functools.partial(slot_kernel, capacity, kv_local, scale),
        grid_spec=pltpu.PrefetchScalarGridSpec(
            num_scalar_prefetch=2,
            grid=(groups,),
            in_specs=[block] + [page_spec(c) for c in range(capacity)],
            out_specs=pl.BlockSpec((1, out_rows, rows, head_dim), lambda g, ids, fill: (g, 0, 0, 0)),
        ),
        out_shape=jax.ShapeDtypeStruct((groups, out_rows, rows, head_dim), jnp.bfloat16),
        compiler_params=pltpu.CompilerParams(vmem_limit_bytes=VMEM_LIMIT),
        cost_estimate=pl.CostEstimate(
            flops=flops, bytes_accessed=64 * 1024 * 1024, transcendentals=flops // (4 * head_dim)
        ),
        name="slot_attention",
    )(slot_pages, slot_fill, slot_queries, page_pool, *([page_pool] * (capacity - 1)))


def hot_kernel(scale, chunk, q_ref, early_ref, late_ref, out_ref, lse_ref):
    rows, head_dim = q_ref.shape[1], q_ref.shape[2]
    pages, page_len = early_ref.shape[0], early_ref.shape[3]
    q = q_ref[0]

    def step(hot_ref, i, carry):
        top, total, mixed = carry
        keys = hot_ref[pl.ds(i * chunk, chunk), 0, 0].reshape(chunk * page_len, head_dim)
        values = hot_ref[pl.ds(i * chunk, chunk), 0, 1].reshape(chunk * page_len, head_dim)
        scores = rows_by_keys(q, keys) * scale
        new_top = jnp.maximum(top, jnp.max(scores, axis=1, keepdims=True))
        weights = jnp.exp(scores - new_top)
        factor = jnp.exp(top - new_top)
        total = total * factor + jnp.sum(weights, axis=1, keepdims=True)
        mixed = mixed * factor + jnp.dot(
            weights.astype(jnp.bfloat16), values, preferred_element_type=jnp.float32
        )
        return new_top, total, mixed

    carry = (
        jnp.full((rows, 1), NEG_FILL, jnp.float32),
        jnp.zeros((rows, 1), jnp.float32),
        jnp.zeros((rows, head_dim), jnp.float32),
    )
    for hot_ref in (early_ref, late_ref):
        carry = lax.fori_loop(
            0, pages // chunk, functools.partial(step, hot_ref), carry, unroll=2
        )
    top, total, mixed = carry
    out_ref[0] = mixed / total
    lse_ref[0] = jnp.broadcast_to(top + jnp.log(total), (rows, 128))


def hot_attention(query_rows, hot_kv, scale):
    kv_local, rows, head_dim = query_rows.shape
    pages, page_len = hot_kv.shape[0], hot_kv.shape[3]
    block = math.gcd(rows, 512)
    flops = 4 * kv_local * rows * pages * page_len * head_dim
    spec = pl.BlockSpec((1, block, head_dim), lambda x, m: (x, m, 0))
    half = (pages // 2, 1, 2, page_len, head_dim)
    early = pl.BlockSpec(half, lambda x, m: (0, x, 0, 0, 0))
    late = pl.BlockSpec(half, lambda x, m: (1, x, 0, 0, 0))
    return pl.pallas_call(
        functools.partial(hot_kernel, scale, math.gcd(pages // 2, 4)),
        grid=(kv_local, rows // block),
        in_specs=[spec, early, late],
        out_specs=[spec, pl.BlockSpec((1, block, 128), lambda x, m: (x, m, 0))],
        out_shape=[
            jax.ShapeDtypeStruct((kv_local, rows, head_dim), jnp.float32),
            jax.ShapeDtypeStruct((kv_local, rows, 128), jnp.float32),
        ],
        compiler_params=pltpu.CompilerParams(vmem_limit_bytes=VMEM_LIMIT),
        cost_estimate=pl.CostEstimate(
            flops=flops, bytes_accessed=16 * 1024 * 1024, transcendentals=flops // (4 * head_dim)
        ),
        name="hot_attention",
    )(query_rows, hot_kv, hot_kv)


def join_kernel(
    max_pages, per_kv, scale, slot_ref, q_ref, fresh_ref, hot_ref, hot_lse_ref, lse_ref, *refs
):
    parts, out_ref = refs[:max_pages], refs[max_pages]
    kv_local, rows, _ = q_ref.shape[1:]
    steps = fresh_ref.shape[3]
    key_step = lax.broadcasted_iota(jnp.int32, (rows, steps), 1)
    row_step = lax.broadcasted_iota(jnp.int32, (rows, steps), 0) // per_kv
    causal = key_step <= row_step
    stats = lse_ref[0]
    for x in range(kv_local):
        fresh = rows_by_keys(q_ref[0, x], fresh_ref[0, x, 0]) * scale
        fresh = jnp.where(causal, fresh, NEG_FILL)
        hot_lse = hot_lse_ref[x][:, :1]
        page_lse = stats[:, x * max_pages : (x + 1) * max_pages]
        top = jnp.maximum(hot_lse, jnp.max(fresh, axis=1, keepdims=True))
        top = jnp.maximum(top, jnp.max(page_lse, axis=1, keepdims=True))
        weights = jnp.where(causal, jnp.exp(fresh - top), 0.0)
        hot_weight = jnp.exp(hot_lse - top)
        shares = jnp.exp(page_lse - top)
        total = jnp.sum(weights, axis=1, keepdims=True) + hot_weight
        total = total + jnp.sum(shares, axis=1, keepdims=True)
        mixed = hot_ref[x] * hot_weight + jnp.dot(
            weights.astype(jnp.bfloat16), fresh_ref[0, x, 1], preferred_element_type=jnp.float32
        )
        for p in range(max_pages):
            mixed = mixed + parts[p][0, x].astype(jnp.float32) * shares[:, p : p + 1]
        out_ref[0, x] = (mixed / total).astype(jnp.bfloat16)


def join(capacity, slot_of, query_rows, fresh_rows, hot_out, hot_lse, page_lse, parts, per_kv, scale):
    requests, kv_local, rows, head_dim = query_rows.shape
    max_pages = slot_of.shape[0] // requests
    steps = fresh_rows.shape[3]

    def part_spec(p):
        return pl.BlockSpec(
            (1, kv_local, rows, head_dim),
            lambda r, slot: (
                lax.div(slot[r * max_pages + p], capacity),
                lax.rem(slot[r * max_pages + p], capacity),
                0,
                0,
            ),
        )

    own = pl.BlockSpec((1, kv_local, rows, head_dim), lambda r, slot: (r, 0, 0, 0))
    return pl.pallas_call(
        functools.partial(join_kernel, max_pages, per_kv, scale),
        grid_spec=pltpu.PrefetchScalarGridSpec(
            num_scalar_prefetch=1,
            grid=(requests,),
            in_specs=[
                own,
                pl.BlockSpec((1, kv_local, 2, steps, head_dim), lambda r, slot: (r, 0, 0, 0, 0)),
                pl.BlockSpec((kv_local, rows, head_dim), lambda r, slot: (0, r, 0)),
                pl.BlockSpec((kv_local, rows, 128), lambda r, slot: (0, r, 0)),
                pl.BlockSpec((1, rows, 128), lambda r, slot: (r, 0, 0)),
            ]
            + [part_spec(p) for p in range(max_pages)],
            out_specs=own,
        ),
        out_shape=jax.ShapeDtypeStruct(query_rows.shape, jnp.bfloat16),
        compiler_params=pltpu.CompilerParams(vmem_limit_bytes=VMEM_LIMIT),
        name="join",
    )(slot_of, query_rows, fresh_rows, hot_out, hot_lse, page_lse, *([parts] * max_pages))


def on_device(
    queries, fresh_kv, page_pool, context_len, page_holder, page_index, hot_owner, hot_pages
):
    requests, steps, local_heads, head_dim = queries.shape
    kv_local = fresh_kv.shape[2]
    per_kv = local_heads // kv_local
    rows = steps * per_kv
    page_len = page_pool.shape[3]
    max_pages = page_holder.shape[1]
    groups = lax.axis_size("group")
    capacity = max(2, (requests * max_pages + groups - 1) // groups)
    slots = groups * capacity
    scale = 1.0 / math.sqrt(head_dim)

    query_rows = queries.reshape(requests, steps, kv_local, per_kv, head_dim)
    query_rows = query_rows.transpose(0, 2, 1, 3, 4).reshape(requests, kv_local, rows, head_dim)
    fresh_rows = fresh_kv.transpose(0, 2, 3, 1, 4)

    hot_kept = kept_by(jnp.take(page_pool, hot_pages, axis=0), "group", hot_owner[0])
    query_rows, hot_kept = lax.optimization_barrier((query_rows, hot_kept))
    hot_share = lax.psum_scatter(
        hot_kept.reshape(-1, head_dim), "group", scatter_dimension=0, tiled=True
    )

    page_start = jnp.arange(max_pages, dtype=jnp.int32)[None, :] * page_len
    filled = jnp.clip(context_len[:, None] - page_start, 0, page_len).reshape(-1)
    live = filled > 0
    holder = page_holder.reshape(-1)
    member = (holder[:, None] == jnp.arange(groups, dtype=jnp.int32)[None, :]) & live[:, None]
    member = member.astype(jnp.int32)
    rank = jnp.sum((jnp.cumsum(member, axis=0) - member) * member, axis=1)
    slot_of = jnp.where(live, holder * capacity + rank, slots)
    taken = slot_of[None, :] == jnp.arange(slots, dtype=jnp.int32)[:, None]

    def by_slot(entry):
        return jnp.sum(jnp.where(taken, entry[None, :], 0), axis=1)

    entry_request = jnp.arange(requests * max_pages, dtype=jnp.int32) // max_pages
    slot_request = by_slot(entry_request)
    slot_info = jnp.stack([by_slot(page_index.reshape(-1)), by_slot(filled)], axis=1)
    slot_info = slot_info.reshape(groups, capacity, 2)

    asked = lax.all_to_all(slot_info, "group", split_axis=0, concat_axis=0, tiled=True)
    sent = jnp.take(query_rows, slot_request, axis=0)
    came = lax.all_to_all(
        sent.reshape(groups, capacity, kv_local, rows, head_dim),
        "group",
        split_axis=0,
        concat_axis=0,
        tiled=True,
    )
    came, hot_share = lax.optimization_barrier((came, hot_share))
    hot_kv = lax.all_gather(hot_share, "group", axis=0, tiled=True).reshape(hot_kept.shape)
    asked = asked.reshape(slots, 2)
    part = slot_attention(asked[:, 0], asked[:, 1], came, page_pool, scale)
    part, hot_kv = lax.optimization_barrier((part, hot_kv))
    part = lax.all_to_all(part, "group", split_axis=0, concat_axis=0, tiled=True)

    hot_rows = query_rows.transpose(1, 0, 2, 3).reshape(kv_local, requests * rows, head_dim)
    hot_out, hot_lse = hot_attention(hot_rows, hot_kv, scale)

    used = jnp.where(live, slot_of, 0)
    lse = jnp.sum(part[:, capacity * kv_local :].astype(jnp.float32), axis=1)
    lse = lse[:, :, : capacity * kv_local].reshape(groups, rows, capacity, kv_local)
    lse = lse.transpose(0, 2, 1, 3).reshape(slots, rows, kv_local)
    lse = jnp.where(live[:, None, None], jnp.take(lse, used, axis=0), NEG_FILL)
    lse = lse.reshape(requests, max_pages, rows, kv_local).transpose(0, 2, 3, 1)
    lse = lse.reshape(requests, rows, max_pages * kv_local)
    lse = jnp.pad(lse, ((0, 0), (0, 0), (0, 128 - max_pages * kv_local)))
    attended = join(
        capacity, used, query_rows, fresh_rows, hot_out, hot_lse, lse, part, per_kv, scale
    )
    attended = attended.reshape(requests, kv_local, steps, per_kv, head_dim)
    return attended.transpose(0, 2, 1, 3, 4).reshape(requests, steps, local_heads, head_dim)


def solution(mesh):
    placed = (
        P("group", None, "head", None),
        P("group", None, "head", None, None),
        P("group", "head", None, None, None),
        P("group"),
        P("group", None),
        P("group", None),
        P(),
        P(),
    )
    return jax.shard_map(
        on_device,
        mesh=mesh,
        in_specs=placed,
        out_specs=P("group", None, "head", None),
        check_vma=False,
    )
```
